128 devices in a mesh: sx: 16 (over z, y_hi, core), sy: 8 (over y_lo, x).
Axes of the slice: x: 4, y: 4 (y_hi: 2, y_lo: 2; y = y_hi * 2 + y_lo), z: 4, core: 2. Of those that a mesh axis runs over, the one named last changes fastest.
Arguments:
- coeffs: float32 [2, 8, 8, 16, 8, 32, 128], P(None, None, None, 'sx', 'sy'), may hold values from -0.9 to 0.9
Outputs:
- traces: float32 [2, 8, 8, 512, 1024], P(None, None, None, 'sx', 'sy')
The draws below stay inside these ranges and needn't reach their ends.
All inputs are finite; a program needn't handle non-finite values.
Results may differ from the reference program's by a relative error of at most 0.0019.
Values sent between devices are 32-bit elements; how exact they have to be, the bound alone decides.
A program may use at most 192 MiB of HBM per device.

```python
import math
import jax
import jax.numpy as jnp
import numpy as np
from jax import lax

N = 8192
Q = 8
TBX = 32
TBY = 128
SRCX = 16
SRCY = 8
LEVX = 4
LEVY = 3
TX = 512
TY = 1024


def levels(key, dims, shards, low, largest):
    def one(dim, shards_of):
        draws = jax.random.uniform(jax.random.fold_in(jax.random.fold_in(key, 6), dim), (shards_of,), jnp.float32, low / len(shards), largest / len(shards))
        return jnp.repeat(jnp.exp(draws), dims[dim] // shards_of).reshape((-1,) + (1,) * (len(dims) - dim - 1))

    gain = one(*shards[0])
    for cut in shards[1:]:
        gain = gain * one(*cut)
    return gain


def scatter_about(own_key, dims, spread, limit, cuts=(), held_as=jnp.bfloat16):
    entries = jax.random.normal(own_key, dims, jnp.float32) * spread
    if len(cuts) > 0:
        entries = levels(own_key, dims, cuts, -0.22, 0.18) * entries
    return jnp.clip(entries, min=-limit, max=limit).astype(held_as)


def setup_inputs(seed: int = 0) -> dict:
    key_list = jax.random.split(jax.random.key(seed), 2)
    return {
        "coeffs": scatter_about(key_list[0], (2, Q, Q, SRCX, SRCY, TBX, TBY), 0.15, 0.9, ((3, 16), (4, 8)), jnp.float32),
    }


def node_list():
    return (1.0 - np.cos(np.pi * (2.0 * np.arange(Q) + 1.0) / (2.0 * Q))) / 2.0

def cheb_table(child_half):
    cheb_nodes = node_list()
    targets = (child_half + cheb_nodes) / 2.0
    lagrange = np.ones((Q, Q))
    for column in range(Q):
        for other_node in range(Q):
            if other_node != column:
                lagrange[:, column] = lagrange[:, column] * (targets - cheb_nodes[other_node]) / (cheb_nodes[column] - cheb_nodes[other_node])
    return jnp.asarray(lagrange, jnp.float32)

def positions(box_index, source_count):
    cheb_nodes = jnp.asarray(node_list(), jnp.float32)
    return (box_index.astype(jnp.float32)[None, :] + cheb_nodes[:, None]) * (4.0 * source_count / N)

def centers(box_index, source_count):
    return (box_index.astype(jnp.float32) + 0.5) * (N / source_count) - 0.5 * N

def phase_gap(spot_one, spot_two, child_one, child_two, parent_one, parent_two):
    place_one = spot_one[:, None, None, None, :, None]
    place_two = spot_two[None, :, None, None, None, :]
    wave_one = child_one[None, None, :, None, None, None]
    wave_two = child_two[None, None, None, :, None, None]
    base_one = parent_one[None, None, :, None, None, None]
    base_two = parent_two[None, None, None, :, None, None]
    two_pi = 2.0 * math.pi
    speed_one = (2.0 + jnp.sin(two_pi * place_one) * jnp.sin(two_pi * place_two)) / 16.0
    speed_two = (2.0 + jnp.cos(two_pi * place_one) * jnp.cos(two_pi * place_two)) / 16.0
    square_one = speed_one * speed_one
    square_two = speed_two * speed_two
    child_root = jnp.sqrt(square_one * wave_one * wave_one + square_two * wave_two * wave_two)
    parent_root = jnp.sqrt(square_one * base_one * base_one + square_two * base_two * base_two)
    linear = place_one * (wave_one - base_one) + place_two * (wave_two - base_two)
    return two_pi * (linear + child_root - parent_root)

def rotate(current, phase_arg, sign_value):
    cosine = jnp.cos(phase_arg)
    sine_part = sign_value * jnp.sin(phase_arg)
    real_part = current[0] * cosine - current[1] * sine_part
    imag_part = current[1] * cosine + current[0] * sine_part
    return jnp.stack([real_part, imag_part])

def interpolate(turned, lagrange, axis_dim):
    if axis_dim == 0:
        return jnp.einsum('ij,zjabcde->ziabcde', lagrange, turned, precision=lax.Precision.HIGHEST)
    return jnp.einsum('ij,zajbcde->zaibcde', lagrange, turned, precision=lax.Precision.HIGHEST)

def level_step(current, axis_dim):
    source_x, source_y, target_x, target_y = current.shape[3:]
    spreads = [interpolate(current, cheb_table(child_half), axis_dim) for child_half in range(2)]
    rows_x = jnp.arange(source_x, dtype=jnp.int32)
    rows_y = jnp.arange(source_y, dtype=jnp.int32)
    child_one = centers(rows_x, source_x)
    child_two = centers(rows_y, source_y)
    if axis_dim == 0:
        joined = jnp.reshape(jnp.stack(spreads, axis=6), (2, Q, Q, source_x, source_y, 2 * target_x, target_y))
        spot_one = positions(jnp.arange(2 * target_x, dtype=jnp.int32), source_x // 2)
        spot_two = positions(jnp.arange(target_y, dtype=jnp.int32), source_y)
        parent_one = centers(rows_x // 2, source_x // 2)
        parent_two = child_two
    else:
        joined = jnp.reshape(jnp.stack(spreads, axis=7), (2, Q, Q, source_x, source_y, target_x, 2 * target_y))
        spot_one = positions(jnp.arange(target_x, dtype=jnp.int32), source_x)
        spot_two = positions(jnp.arange(2 * target_y, dtype=jnp.int32), source_y // 2)
        parent_one = child_one
        parent_two = centers(rows_y // 2, source_y // 2)
    turned = rotate(joined, phase_gap(spot_one, spot_two, child_one, child_two, parent_one, parent_two), 1.0)
    wide_x, wide_y = turned.shape[5:]
    if axis_dim == 0:
        halves = jnp.reshape(turned, (2, Q, Q, source_x // 2, 2, source_y, wide_x, wide_y))
        return halves[:, :, :, :, 0] + halves[:, :, :, :, 1]
    halves = jnp.reshape(turned, (2, Q, Q, source_x, source_y // 2, 2, wide_x, wide_y))
    return halves[:, :, :, :, :, 0] + halves[:, :, :, :, :, 1]

def reference(coeffs):
    current = coeffs
    for height in range(LEVX):
        current = level_step(current, 0)
    for height in range(LEVY):
        current = level_step(current, 1)
    return jnp.reshape(current, (2, Q, Q, TX, TY))
```

```python
import functools
import math

import jax
import jax.numpy as jnp
import numpy as np
from jax import lax
from jax.experimental import pallas as pl
from jax.experimental.pallas import tpu as pltpu
from jax.sharding import PartitionSpec as P

N = 8192
Q = 8
DX = 16
DY = 8
LX = 4
LY = 3
ROWS = 8
CHUNKS = 2
LANES = 128
MESH = pl.DeviceIdType.MESH


def node_list():
    return (1.0 - np.cos(np.pi * (2.0 * np.arange(Q) + 1.0) / (2.0 * Q))) / 2.0


def cheb_table(child_half):
    nodes = node_list()
    targets = (child_half + nodes) / 2.0
    table = np.ones((Q, Q))
    for m in range(Q):
        for n in range(Q):
            if n != m:
                table[:, m] = table[:, m] * (targets - nodes[n]) / (nodes[m] - nodes[n])
    return table


def spread_weights(axis):
    eye = np.eye(Q)
    parts = []
    for h in range(2):
        table = cheb_table(h).T
        block = np.kron(table, eye) if axis == 0 else np.kron(eye, table)
        parts.append(np.kron(np.eye(2), block))
    full = np.concatenate(parts, axis=1).astype(np.float32)
    high = full.astype(jnp.bfloat16)
    low = (full - high.astype(np.float32)).astype(jnp.bfloat16)
    return np.concatenate([high, high], axis=0), low


def lane_table():
    z = node_list()
    lane = np.arange(LANES)
    z_one = z[(lane // Q) % Q]
    z_two = z[lane % Q]
    rows = [
        z_one,
        z_two,
        (lane // (Q * Q)).astype(np.float64),
        np.cos(2 * np.pi * z_one),
        np.sin(2 * np.pi * z_one),
        np.cos(2 * np.pi * z_two),
        np.sin(2 * np.pi * z_two),
        np.zeros(LANES),
    ]
    return np.stack(rows).astype(np.float32)


def fit(function, count, odd):
    r = 0.5 * np.cos(np.pi * (np.arange(400) + 0.5) / 800)
    basis = np.stack([r ** (2 * k + (1 if odd else 0)) for k in range(count)], axis=1)
    return [float(c) for c in np.linalg.lstsq(basis, function(r), rcond=None)[0]]


SIN_FIT = fit(lambda r: 2.0 * np.sin(np.pi * r), 5, True)
COS_FIT = fit(lambda r: np.cos(np.pi * r), 5, False)


def horner(coefs, z):
    total = coefs[-1] * z + coefs[-2]
    for c in coefs[-3::-1]:
        total = total * z + c
    return total


def turn(cycles):
    r = cycles - jnp.round(cycles)
    z = r * r
    twice_sine = horner(SIN_FIT, z) * r
    cosine = horner(COS_FIT, z)
    return 1.0 - 0.5 * (twice_sine * twice_sine), twice_sine * cosine


def root(v):
    inverse = lax.rsqrt(v)
    s = v * inverse
    return s + (0.5 * inverse) * (v - s * s), inverse


def with_linear(cosine, sine, lin_cos, lin_sin):
    rc = cosine * lin_cos
    ss = sine * lin_sin
    rs = cosine * lin_sin
    sc = sine * lin_cos
    return rc + ss, sc - rs, rc - ss, sc + rs


def kernel(
    x_hbm,
    lane_ref,
    wx_high,
    wx_low,
    wy_high,
    wy_low,
    out_ref,
    x_ref,
    send_buf,
    recv_buf,
    state_a,
    state_b,
    fin,
    tw_x,
    tw_y0,
    tw_y1,
    tw_y2,
    c2_tab,
    load_sem,
    send_sem,
    recv_sem,
):
    ix = lax.axis_index("sx")
    iy = lax.axis_index("sy")
    slots = DX * DY

    load = pltpu.make_async_copy(x_hbm, x_ref, load_sem)
    load.start()

    barrier = pltpu.get_barrier_semaphore()

    def greet(j, carry):
        other = (lax.rem(ix + j // DY, DX), lax.rem(iy + lax.rem(j, DY), DY))
        pl.semaphore_signal(barrier, inc=1, device_id=other, device_id_type=MESH)
        return carry

    lax.fori_loop(1, slots, greet, 0)
    load.wait()

    def pack(dx):
        for part in range(2):
            halves = [
                x_ref[pl.ds(part * 2048 + 2 * dx + g, Q * Q, stride=32), :] for g in range(2)
            ]
            turned = jnp.concatenate(halves, axis=0).T
            for dy in range(DY):
                for c in range(CHUNKS):
                    low = (dy * CHUNKS + c) * ROWS
                    send_buf[c, dx * DY + dy, part] = turned[low : low + ROWS]

    def send(c, dx, dy):
        pltpu.make_async_remote_copy(
            src_ref=send_buf.at[c, dx * DY + dy],
            dst_ref=recv_buf.at[c, iy * DX + ix],
            send_sem=send_sem.at[c],
            recv_sem=recv_sem.at[c],
            device_id=(dx, dy),
            device_id_type=MESH,
        ).start()

    pack(ix)
    for c in range(CHUNKS):
        recv_buf[c, iy * DX + ix] = send_buf[c, ix * DY + iy]
    pl.semaphore_wait(barrier, slots - 1)
    for jy in range(1, DY):
        send(0, ix, lax.rem(iy + jy, DY))

    def pack_and_send(jx, carry):
        dx = lax.rem(ix + jx, DX)
        pack(dx)
        for jy in range(DY):
            send(0, dx, lax.rem(iy + jy, DY))
        return carry

    lax.fori_loop(1, DX, pack_and_send, 0)

    def send_later(j, carry):
        send(1, lax.rem(ix + j // DY, DX), lax.rem(iy + lax.rem(j, DY), DY))
        return carry

    lax.fori_loop(1, slots, send_later, 0)

    z_one = lane_ref[0:1, :]
    z_two = lane_ref[1:2, :]
    g_bit = lane_ref[2:3, :]
    cos_one, sin_one = lane_ref[3:4, :], lane_ref[4:5, :]
    cos_two, sin_two = lane_ref[5:6, :], lane_ref[6:7, :]
    row = lax.broadcasted_iota(jnp.int32, (ROWS, LANES), 0).astype(jnp.float32)
    base_one = (2 * ix).astype(jnp.float32) + g_bit

    def place_one(level, h):
        box = base_one * float(2 << level) + h.astype(jnp.float32)
        count = DX >> (level + 1)
        return jnp.broadcast_to((box + z_one) * (4.0 * count / N), (ROWS, LANES))

    def place_two(c, level, h):
        box = (row + (iy * (CHUNKS * ROWS) + c * ROWS).astype(jnp.float32)) * float(1 << level) + float(h)
        count = DY >> level
        return (box + z_two) * (4.0 * count / N)

    for level in range(LX):
        count = DX >> level
        width = N // count
        fans = 2 << level

        def x_twiddles(step, carry, level=level, count=count, width=width, fans=fans):
            c = step // fans
            h = lax.rem(step, fans)
            c1, s1 = turn(place_one(level, h))
            c2, s2 = turn(place_two(c, 0, 0))
            speed_one = (2.0 + s1 * s2) * (1.0 / 16.0)
            speed_two = (2.0 + c1 * c2) * (1.0 / 16.0)
            square_one = speed_one * speed_one
            square_two = speed_two * speed_two
            for u2 in range(DY // 2):
                k2 = (u2 + 0.5) * (N / DY) - 0.5 * N
                second = square_two * (k2 * k2)
                parents = {}
                for u1 in range(count // 2):
                    child = (u1 + 0.5) * width - 0.5 * N
                    parent = (u1 // 2 + 0.5) * (2 * width) - 0.5 * N
                    if parent not in parents:
                        parents[parent] = root(square_one * (parent * parent) + second)[0]
                    s_parent = parents[parent]
                    s_child, _ = root(square_one * (child * child) + second)
                    total = s_child + s_parent
                    gap = square_one * (child * child - parent * parent) / total
                    cosine, sine = turn(gap)
                    four = with_linear(cosine, sine, cos_one, sin_one)
                    for k in range(4):
                        tw_x[level, c, u2, u1 * fans + h, k] = four[k]
            return carry

        lax.fori_loop(0, CHUNKS * fans, x_twiddles, 0)

    for c in range(CHUNKS):
        for level in range(LY):
            for h in range(2 << level):
                cosine, _ = turn(place_two(c, level + 1, h))
                c2_tab[c, (2 << level) - 2 + h] = cosine

    tw_y = (tw_y0, tw_y1, tw_y2)

    def y_twiddles(step, carry):
        c = step // DX
        h = lax.rem(step, DX)
        c1, _ = turn(place_one(LX - 1, h))
        for level in range(LY):
            for k in range(2 << level):
                gap = c1 * c2_tab[c, (2 << level) - 2 + k] * float((N // 16 << level) // 16)
                cosine, sine = turn(gap)
                four = with_linear(cosine, sine, cos_two, sin_two)
                for q in range(4):
                    tw_y[level][c, h, k, q] = four[q]
        return carry

    lax.fori_loop(0, CHUNKS * DX, y_twiddles, 0)

    def spread(block, high_ref, low_ref):
        high = block.astype(jnp.bfloat16)
        low = (block - high.astype(jnp.float32)).astype(jnp.bfloat16)
        both = jnp.concatenate([high, low], axis=1)
        main = jnp.dot(both, high_ref[...], preferred_element_type=jnp.float32)
        return main + jnp.dot(high, low_ref[...], preferred_element_type=jnp.float32)

    def levels(c, carry):
        pltpu.make_async_remote_copy(
            src_ref=send_buf.at[c, pl.ds(0, slots - 1)],
            dst_ref=recv_buf.at[c, pl.ds(0, slots - 1)],
            send_sem=send_sem.at[c],
            recv_sem=recv_sem.at[c],
            device_id=(ix, iy),
            device_id_type=MESH,
        ).wait_recv()

        for level in range(LX):
            count = DX >> level
            fans = 1 << level
            source = (None, state_a, state_b, state_a)[level]
            target = (state_a, state_b, state_a, state_b)[level]

            def x_level(b2, carry, level=level, count=count, fans=fans, source=source, target=target):
                if level == 0:
                    block = recv_buf[c, pl.ds(b2 * DX, DX)]
                else:
                    block = source[pl.ds(b2 * DX, DX)]
                wide = spread(block.reshape(DX * 2 * ROWS, LANES), wx_high, wx_low)
                u2 = jnp.minimum(b2, DY - 1 - b2)
                for parent in range(count // 2):
                    for old in range(fans):
                        for h in range(2):
                            fan = 2 * old + h
                            re = im = None
                            for bit in range(2):
                                b1 = 2 * parent + bit
                                u1 = min(b1, count - 1 - b1)
                                low = (b1 * fans + old) * 2 * ROWS
                                a_re = wide[low : low + ROWS, h * LANES : (h + 1) * LANES]
                                a_im = wide[low + ROWS : low + 2 * ROWS, h * LANES : (h + 1) * LANES]
                                t_re = tw_x[level, c, u2, u1 * 2 * fans + fan, 2 * bit]
                                t_im = tw_x[level, c, u2, u1 * 2 * fans + fan, 2 * bit + 1]
                                n_re = a_re * t_re - a_im * t_im
                                n_im = a_re * t_im + a_im * t_re
                                re = n_re if re is None else re + n_re
                                im = n_im if im is None else im + n_im
                            slot = parent * 2 * fans + fan
                            if level == LX - 1:
                                target[slot * DY + b2, 0] = re
                                target[slot * DY + b2, 1] = im
                            else:
                                target[b2 * DX + slot, 0] = re
                                target[b2 * DX + slot, 1] = im
                return carry

            lax.fori_loop(0, DY, x_level, 0)

        for level in range(LY):
            count = DY >> level
            fans = 1 << level
            source = (state_b, state_a, state_b)[level]
            target = (state_a, state_b, None)[level]
            table = tw_y[level]

            def y_level(pair, carry, level=level, count=count, fans=fans, source=source, target=target, table=table):
                block = source[pl.ds(pair * 2 * DY, 2 * DY)]
                wide = spread(block.reshape(2 * DY * 2 * ROWS, LANES), wy_high, wy_low)
                for which in range(2):
                    hx = pair * 2 + which
                    for old in range(fans):
                        for h in range(2):
                            fan = 2 * old + h
                            u_re, u_im, w_re, w_im = (table[c, hx, fan, q] for q in range(4))
                            cut = slice(h * LANES, (h + 1) * LANES)
                            for parent in range(count // 2):
                                low_a = (which * DY + 2 * parent * fans + old) * 2 * ROWS
                                low_b = (which * DY + (2 * parent + 1) * fans + old) * 2 * ROWS
                                a_re = wide[low_a : low_a + ROWS, cut]
                                a_im = wide[low_a + ROWS : low_a + 2 * ROWS, cut]
                                b_re = wide[low_b : low_b + ROWS, cut]
                                b_im = wide[low_b + ROWS : low_b + 2 * ROWS, cut]
                                if level == LY - 1:
                                    re = (a_re * u_re - a_im * u_im) + (b_re * w_re - b_im * w_im)
                                    im = (a_re * u_im + a_im * u_re) + (b_re * w_im + b_im * w_re)
                                elif parent < count // 4:
                                    re = (a_re + b_re) * u_re - (a_im - b_im) * u_im
                                    im = (a_im + b_im) * u_re + (a_re - b_re) * u_im
                                else:
                                    re = (a_re + b_re) * w_re + (a_im - b_im) * w_im
                                    im = (a_im + b_im) * w_re - (a_re - b_re) * w_im
                                if level == LY - 1:
                                    fin[0, hx, pl.ds(c * (ROWS * DY) + fan, ROWS, stride=DY), :] = re
                                    fin[1, hx, pl.ds(c * (ROWS * DY) + fan, ROWS, stride=DY), :] = im
                                else:
                                    slot = hx * DY + parent * 2 * fans + fan
                                    target[slot, 0] = re
                                    target[slot, 1] = im
                return carry

            lax.fori_loop(0, DX // 2, y_level, 0)
        return carry

    lax.fori_loop(0, CHUNKS, levels, 0)

    def unpack(hx, carry):
        for part in range(2):
            turned = fin[part, hx].T
            for g in range(2):
                out_ref[pl.ds(part * 2048 + g * DX + hx, Q * Q, stride=32), :] = turned[
                    g * Q * Q : (g + 1) * Q * Q
                ]
        return carry

    lax.fori_loop(0, DX, unpack, 0)

    for c in range(CHUNKS):
        pltpu.make_async_remote_copy(
            src_ref=send_buf.at[c, pl.ds(0, slots - 1)],
            dst_ref=recv_buf.at[c, pl.ds(0, slots - 1)],
            send_sem=send_sem.at[c],
            recv_sem=recv_sem.at[c],
            device_id=(ix, iy),
            device_id_type=MESH,
        ).wait_send()


def local(coeffs):
    rows = 2 * Q * Q * 32
    flat = jnp.reshape(coeffs, (rows, LANES))
    wx_high, wx_low = spread_weights(0)
    wy_high, wy_low = spread_weights(1)
    vmem = pl.BlockSpec(memory_space=pltpu.VMEM)
    slots = DX * DY
    f32 = jnp.float32
    out = pl.pallas_call(
        kernel,
        out_shape=jax.ShapeDtypeStruct((rows, LANES), f32),
        in_specs=[pl.BlockSpec(memory_space=pl.ANY)] + [vmem] * 5,
        out_specs=vmem,
        scratch_shapes=[
            pltpu.VMEM((rows, LANES), f32),
            pltpu.VMEM((CHUNKS, slots, 2, ROWS, LANES), f32),
            pltpu.VMEM((CHUNKS, slots, 2, ROWS, LANES), f32),
            pltpu.VMEM((slots, 2, ROWS, LANES), f32),
            pltpu.VMEM((slots, 2, ROWS, LANES), f32),
            pltpu.VMEM((2, DX, LANES, LANES), f32),
            pltpu.VMEM((LX, CHUNKS, DY // 2, DX, 4, ROWS, LANES), f32),
            pltpu.VMEM((CHUNKS, DX, 2, 4, ROWS, LANES), f32),
            pltpu.VMEM((CHUNKS, DX, 4, 4, ROWS, LANES), f32),
            pltpu.VMEM((CHUNKS, DX, 8, 4, ROWS, LANES), f32),
            pltpu.VMEM((CHUNKS, 14, ROWS, LANES), f32),
            pltpu.SemaphoreType.DMA,
            pltpu.SemaphoreType.DMA((CHUNKS,)),
            pltpu.SemaphoreType.DMA((CHUNKS,)),
        ],
        compiler_params=pltpu.CompilerParams(
            collective_id=0, has_side_effects=True, vmem_limit_bytes=56 << 20
        ),
        name="butterfly",
    )(
        flat,
        jnp.asarray(lane_table()),
        jnp.asarray(wx_high),
        jnp.asarray(wx_low),
        jnp.asarray(wy_high),
        jnp.asarray(wy_low),
    )
    return jnp.reshape(out, (2, Q, Q, 32, LANES))


def solution(mesh):
    in_specs = (P(None, None, None, "sx", "sy", None, None),)
    out_specs = P(None, None, None, "sx", "sy")
    return jax.shard_map(local, mesh=mesh, in_specs=in_specs, out_specs=out_specs, check_vma=False)
```

```python
import functools
import math

import jax
import jax.numpy as jnp
import numpy as np
from jax import lax
from jax.experimental import pallas as pl
from jax.experimental.pallas import tpu as pltpu
from jax.sharding import PartitionSpec as P

N = 8192
Q = 8
DX = 16
DY = 8
LX = 4
LY = 3
ROWS = 8
CHUNKS = 2
LANES = 128
MESH = pl.DeviceIdType.MESH


def node_list():
    return (1.0 - np.cos(np.pi * (2.0 * np.arange(Q) + 1.0) / (2.0 * Q))) / 2.0


def cheb_table(child_half):
    nodes = node_list()
    targets = (child_half + nodes) / 2.0
    table = np.ones((Q, Q))
    for m in range(Q):
        for n in range(Q):
            if n != m:
                table[:, m] = table[:, m] * (targets - nodes[n]) / (nodes[m] - nodes[n])
    return table


def pick(index, values):
    total = jnp.full(index.shape, float(values[0]), jnp.float32)
    for k in range(1, len(values)):
        total = jnp.where(index == k, float(values[k]), total)
    return total


def fill_weights(axis, high_ref, low_ref):
    nodes = node_list()
    scale = [1.0 / np.prod([nodes[m] - nodes[n] for n in range(Q) if n != m]) for m in range(Q)]
    shape = (LANES, 2 * LANES)
    source = lax.broadcasted_iota(jnp.int32, (LANES, 1), 0)
    target = lax.broadcasted_iota(jnp.int32, (1, 2 * LANES), 1)
    first, second = source // Q % Q, source % Q
    t_first, t_second = target // Q % Q, target % Q
    child = (target // LANES).astype(jnp.float32)
    if axis == 0:
        own, other, t_own, t_other = first, second, t_first, t_second
    else:
        own, other, t_own, t_other = second, first, t_second, t_first
    place = (child + pick(t_own, nodes)) * 0.5
    table = jnp.broadcast_to(pick(own, scale), shape)
    for n in range(Q):
        table = table * jnp.where(own == n, 1.0, place - float(nodes[n]))
    group = source // (Q * Q) * Q + other
    t_group = target % LANES // (Q * Q) * Q + t_other
    table = jnp.where(group == t_group, table, 0.0)
    high = table.astype(jnp.bfloat16)
    high_ref[0:LANES, :] = high
    high_ref[LANES : 2 * LANES, :] = high
    low_ref[...] = (table - high.astype(jnp.float32)).astype(jnp.bfloat16)


def fit(function, count, odd):
    r = 0.5 * np.cos(np.pi * (np.arange(400) + 0.5) / 800)
    basis = np.stack([r ** (2 * k + (1 if odd else 0)) for k in range(count)], axis=1)
    return [float(c) for c in np.linalg.lstsq(basis, function(r), rcond=None)[0]]


SIN_FIT = fit(lambda r: 2.0 * np.sin(np.pi * r), 5, True)
COS_FIT = fit(lambda r: np.cos(np.pi * r), 5, False)


def horner(coefs, z):
    total = coefs[-1] * z + coefs[-2]
    for c in coefs[-3::-1]:
        total = total * z + c
    return total


def turn(cycles):
    r = cycles - jnp.round(cycles)
    z = r * r
    twice_sine = horner(SIN_FIT, z) * r
    cosine = horner(COS_FIT, z)
    return 1.0 - 0.5 * (twice_sine * twice_sine), twice_sine * cosine


def root(v):
    inverse = lax.rsqrt(v)
    s = v * inverse
    return s + (0.5 * inverse) * (v - s * s), inverse


def with_linear(cosine, sine, lin_cos, lin_sin):
    rc = cosine * lin_cos
    ss = sine * lin_sin
    rs = cosine * lin_sin
    sc = sine * lin_cos
    return rc + ss, sc - rs, rc - ss, sc + rs


def kernel(
    x_hbm,
    out_ref,
    x_ref,
    wx_high,
    wx_low,
    wy_high,
    wy_low,
    send_buf,
    recv_buf,
    state_a,
    state_b,
    fin,
    tw_x,
    tw_y0,
    tw_y1,
    tw_y2,
    c2_tab,
    load_sem,
    send_sem,
    recv_sem,
    row_sem,
):
    ix = lax.axis_index("sx")
    iy = lax.axis_index("sy")
    slots = DX * DY

    load = pltpu.make_async_copy(x_hbm, x_ref, load_sem)
    load.start()

    barrier = pltpu.get_barrier_semaphore()

    def other_x(j):
        return lax.rem(ix + j, DX)

    def other_y(j):
        return lax.rem(iy + j, DY)

    def greet(semaphore, device):
        pl.semaphore_signal(semaphore, inc=1, device_id=device, device_id_type=MESH)

    for j in range(1, DX):
        greet(barrier, (other_x(j), iy))
    for j in range(1, DY):
        greet(barrier, (ix, other_y(j)))
    load.wait()

    def pack(dx):
        for part in range(2):
            halves = [
                x_ref[pl.ds(part * 2048 + 2 * dx + g, Q * Q, stride=32), :] for g in range(2)
            ]
            turned = jnp.concatenate(halves, axis=0).T
            for dy in range(DY):
                for c in range(CHUNKS):
                    low = (dy * CHUNKS + c) * ROWS
                    send_buf[c, dx * DY + dy, part] = turned[low : low + ROWS]

    def send(c, dx, dy):
        pltpu.make_async_remote_copy(
            src_ref=send_buf.at[c, dx * DY + dy],
            dst_ref=recv_buf.at[c, iy * DX + ix],
            send_sem=send_sem.at[c],
            recv_sem=recv_sem.at[c],
            device_id=(dx, dy),
            device_id_type=MESH,
        ).start()

    def sent(c):
        return pltpu.make_async_remote_copy(
            src_ref=send_buf.at[c, pl.ds(0, slots - 1)],
            dst_ref=recv_buf.at[c, pl.ds(0, slots - 1)],
            send_sem=send_sem.at[c],
            recv_sem=recv_sem.at[c],
            device_id=(ix, iy),
            device_id_type=MESH,
        )

    def pack_all(j, carry):
        pack(j)
        return carry

    lax.fori_loop(0, DX, pack_all, 0)
    for c in range(CHUNKS):
        recv_buf[c, iy * DX + ix] = send_buf[c, ix * DY + iy]

    pl.semaphore_wait(barrier, DX + DY - 2)
    for j in range(1, DY):
        greet(row_sem, (ix, other_y(j)))
    for j in range(1, DY):
        send(0, ix, other_y(j))
    for j in range(1, DX):
        send(0, other_x(j), iy)
    pl.semaphore_wait(row_sem, DY - 1)

    def send_rest(j, carry):
        for k in range(1, DY):
            send(0, other_x(j), other_y(k))
        return carry

    lax.fori_loop(1, DX, send_rest, 0)

    fill_weights(0, wx_high, wx_low)
    fill_weights(1, wy_high, wy_low)
    nodes = node_list()
    angles = 2.0 * np.pi * nodes
    lane = lax.broadcasted_iota(jnp.int32, (1, LANES), 1)
    t_one, t_two = lane // Q % Q, lane % Q
    z_one, z_two = pick(t_one, nodes), pick(t_two, nodes)
    cos_one, sin_one = pick(t_one, np.cos(angles)), pick(t_one, np.sin(angles))
    cos_two, sin_two = pick(t_two, np.cos(angles)), pick(t_two, np.sin(angles))
    g_bit = (lane // (Q * Q)).astype(jnp.float32)
    row = lax.broadcasted_iota(jnp.int32, (ROWS, LANES), 0).astype(jnp.float32)
    base_one = (2 * ix).astype(jnp.float32) + g_bit

    def place_one(level, h):
        box = base_one * float(2 << level) + h.astype(jnp.float32)
        count = DX >> (level + 1)
        return jnp.broadcast_to((box + z_one) * (4.0 * count / N), (ROWS, LANES))

    def place_two(c, level, h):
        box = (row + (iy * (CHUNKS * ROWS) + c * ROWS).astype(jnp.float32)) * float(1 << level) + float(h)
        count = DY >> level
        return (box + z_two) * (4.0 * count / N)

    for level in range(LX):
        count = DX >> level
        width = N // count
        fans = 2 << level

        def x_twiddles(step, carry, level=level, count=count, width=width, fans=fans):
            c = step // fans
            h = lax.rem(step, fans)
            c1, s1 = turn(place_one(level, h))
            c2, s2 = turn(place_two(c, 0, 0))
            speed_one = (2.0 + s1 * s2) * (1.0 / 16.0)
            speed_two = (2.0 + c1 * c2) * (1.0 / 16.0)
            square_one = speed_one * speed_one
            square_two = speed_two * speed_two
            for u2 in range(DY // 2):
                k2 = (u2 + 0.5) * (N / DY) - 0.5 * N
                second = square_two * (k2 * k2)
                parents = {}
                for u1 in range(count // 2):
                    child = (u1 + 0.5) * width - 0.5 * N
                    parent = (u1 // 2 + 0.5) * (2 * width) - 0.5 * N
                    if parent not in parents:
                        parents[parent] = root(square_one * (parent * parent) + second)[0]
                    s_parent = parents[parent]
                    s_child, _ = root(square_one * (child * child) + second)
                    total = s_child + s_parent
                    gap = square_one * (child * child - parent * parent) / total
                    cosine, sine = turn(gap)
                    four = with_linear(cosine, sine, cos_one, sin_one)
                    for k in range(4):
                        tw_x[level, c, u2, u1 * fans + h, k] = four[k]
            return carry

        lax.fori_loop(0, CHUNKS * fans, x_twiddles, 0)

    for c in range(CHUNKS):
        for level in range(LY):
            for h in range(2 << level):
                cosine, _ = turn(place_two(c, level + 1, h))
                c2_tab[c, (2 << level) - 2 + h] = cosine

    tw_y = (tw_y0, tw_y1, tw_y2)

    def y_twiddles(step, carry):
        c = step // DX
        h = lax.rem(step, DX)
        c1, _ = turn(place_one(LX - 1, h))
        for level in range(LY):
            for k in range(2 << level):
                gap = c1 * c2_tab[c, (2 << level) - 2 + k] * float((N // 16 << level) // 16)
                cosine, sine = turn(gap)
                four = with_linear(cosine, sine, cos_two, sin_two)
                for q in range(4):
                    tw_y[level][c, h, k, q] = four[q]
        return carry

    lax.fori_loop(0, CHUNKS * DX, y_twiddles, 0)

    sent(0).wait_send()

    def send_second(j, carry):
        send(1, other_x(j // DY), other_y(lax.rem(j, DY)))
        return carry

    lax.fori_loop(1, slots, send_second, 0)

    def spread(block, high_ref, low_ref):
        high = block.astype(jnp.bfloat16)
        low = (block - high.astype(jnp.float32)).astype(jnp.bfloat16)
        both = jnp.concatenate([high, low], axis=1)
        main = jnp.dot(both, high_ref[...], preferred_element_type=jnp.float32)
        return main + jnp.dot(high, low_ref[...], preferred_element_type=jnp.float32)

    def levels(c, carry):
        sent(c).wait_recv()

        for level in range(LX):
            count = DX >> level
            fans = 1 << level
            source = (None, state_a, state_b, state_a)[level]
            target = (state_a, state_b, state_a, state_b)[level]

            def x_level(b2, carry, level=level, count=count, fans=fans, source=source, target=target):
                if level == 0:
                    block = recv_buf[c, pl.ds(b2 * DX, DX)]
                else:
                    block = source[pl.ds(b2 * DX, DX)]
                wide = spread(block.reshape(DX * 2 * ROWS, LANES), wx_high, wx_low)
                u2 = jnp.minimum(b2, DY - 1 - b2)
                for parent in range(count // 2):
                    for old in range(fans):
                        for h in range(2):
                            fan = 2 * old + h
                            re = im = None
                            for bit in range(2):
                                b1 = 2 * parent + bit
                                u1 = min(b1, count - 1 - b1)
                                low = (b1 * fans + old) * 2 * ROWS
                                a_re = wide[low : low + ROWS, h * LANES : (h + 1) * LANES]
                                a_im = wide[low + ROWS : low + 2 * ROWS, h * LANES : (h + 1) * LANES]
                                t_re = tw_x[level, c, u2, u1 * 2 * fans + fan, 2 * bit]
                                t_im = tw_x[level, c, u2, u1 * 2 * fans + fan, 2 * bit + 1]
                                n_re = a_re * t_re - a_im * t_im
                                n_im = a_re * t_im + a_im * t_re
                                re = n_re if re is None else re + n_re
                                im = n_im if im is None else im + n_im
                            slot = parent * 2 * fans + fan
                            if level == LX - 1:
                                target[slot * DY + b2, 0] = re
                                target[slot * DY + b2, 1] = im
                            else:
                                target[b2 * DX + slot, 0] = re
                                target[b2 * DX + slot, 1] = im
                return carry

            lax.fori_loop(0, DY, x_level, 0, unroll=True)

        for level in range(LY):
            count = DY >> level
            fans = 1 << level
            source = (state_b, state_a, state_b)[level]
            target = (state_a, state_b, None)[level]
            table = tw_y[level]

            def y_level(pair, carry, level=level, count=count, fans=fans, source=source, target=target, table=table):
                block = source[pl.ds(pair * 2 * DY, 2 * DY)]
                wide = spread(block.reshape(2 * DY * 2 * ROWS, LANES), wy_high, wy_low)
                for which in range(2):
                    hx = pair * 2 + which
                    for old in range(fans):
                        for h in range(2):
                            fan = 2 * old + h
                            u_re, u_im, w_re, w_im = (table[c, hx, fan, q] for q in range(4))
                            cut = slice(h * LANES, (h + 1) * LANES)
                            for parent in range(count // 2):
                                low_a = (which * DY + 2 * parent * fans + old) * 2 * ROWS
                                low_b = (which * DY + (2 * parent + 1) * fans + old) * 2 * ROWS
                                a_re = wide[low_a : low_a + ROWS, cut]
                                a_im = wide[low_a + ROWS : low_a + 2 * ROWS, cut]
                                b_re = wide[low_b : low_b + ROWS, cut]
                                b_im = wide[low_b + ROWS : low_b + 2 * ROWS, cut]
                                if level == LY - 1:
                                    re = (a_re * u_re - a_im * u_im) + (b_re * w_re - b_im * w_im)
                                    im = (a_re * u_im + a_im * u_re) + (b_re * w_im + b_im * w_re)
                                elif parent < count // 4:
                                    re = (a_re + b_re) * u_re - (a_im - b_im) * u_im
                                    im = (a_im + b_im) * u_re + (a_re - b_re) * u_im
                                else:
                                    re = (a_re + b_re) * w_re + (a_im - b_im) * w_im
                                    im = (a_im + b_im) * w_re - (a_re - b_re) * w_im
                                if level == LY - 1:
                                    fin[0, hx, pl.ds(c * (ROWS * DY) + fan, ROWS, stride=DY), :] = re
                                    fin[1, hx, pl.ds(c * (ROWS * DY) + fan, ROWS, stride=DY), :] = im
                                else:
                                    slot = hx * DY + parent * 2 * fans + fan
                                    target[slot, 0] = re
                                    target[slot, 1] = im
                return carry

            lax.fori_loop(0, DX // 2, y_level, 0, unroll=True)
        return carry

    lax.fori_loop(0, CHUNKS, levels, 0)

    def unpack(hx, carry):
        for part in range(2):
            turned = fin[part, hx].T
            for g in range(2):
                out_ref[pl.ds(part * 2048 + g * DX + hx, Q * Q, stride=32), :] = turned[
                    g * Q * Q : (g + 1) * Q * Q
                ]
        return carry

    lax.fori_loop(0, DX, unpack, 0)

    sent(1).wait_send()


def local(coeffs):
    rows = 2 * Q * Q * 32
    flat = jnp.reshape(coeffs, (rows, LANES))
    slots = DX * DY
    f32 = jnp.float32
    out = pl.pallas_call(
        kernel,
        out_shape=jax.ShapeDtypeStruct((rows, LANES), f32),
        in_specs=[pl.BlockSpec(memory_space=pltpu.HBM)],
        out_specs=pl.BlockSpec(memory_space=pltpu.VMEM),
        scratch_shapes=[
            pltpu.VMEM((rows, LANES), f32),
            pltpu.VMEM((2 * LANES, 2 * LANES), jnp.bfloat16),
            pltpu.VMEM((LANES, 2 * LANES), jnp.bfloat16),
            pltpu.VMEM((2 * LANES, 2 * LANES), jnp.bfloat16),
            pltpu.VMEM((LANES, 2 * LANES), jnp.bfloat16),
            pltpu.VMEM((CHUNKS, slots, 2, ROWS, LANES), f32),
            pltpu.VMEM((CHUNKS, slots, 2, ROWS, LANES), f32),
            pltpu.VMEM((slots, 2, ROWS, LANES), f32),
            pltpu.VMEM((slots, 2, ROWS, LANES), f32),
            pltpu.VMEM((2, DX, LANES, LANES), f32),
            pltpu.VMEM((LX, CHUNKS, DY // 2, DX, 4, ROWS, LANES), f32),
            pltpu.VMEM((CHUNKS, DX, 2, 4, ROWS, LANES), f32),
            pltpu.VMEM((CHUNKS, DX, 4, 4, ROWS, LANES), f32),
            pltpu.VMEM((CHUNKS, DX, 8, 4, ROWS, LANES), f32),
            pltpu.VMEM((CHUNKS, 14, ROWS, LANES), f32),
            pltpu.SemaphoreType.DMA,
            pltpu.SemaphoreType.DMA((CHUNKS,)),
            pltpu.SemaphoreType.DMA((CHUNKS,)),
            pltpu.SemaphoreType.REGULAR,
        ],
        compiler_params=pltpu.CompilerParams(
            collective_id=0, has_side_effects=True, vmem_limit_bytes=32 << 20
        ),
        name="butterfly",
    )(flat)
    return jnp.reshape(out, (2, Q, Q, 32, LANES))


def solution(mesh):
    in_specs = (P(None, None, None, "sx", "sy", None, None),)
    out_specs = P(None, None, None, "sx", "sy")
    return jax.shard_map(local, mesh=mesh, in_specs=in_specs, out_specs=out_specs, check_vma=False)
```

```python
import functools
import math

import jax
import jax.numpy as jnp
import numpy as np
from jax import lax
from jax.experimental import pallas as pl
from jax.experimental.pallas import tpu as pltpu
from jax.sharding import PartitionSpec as P

N = 8192
Q = 8
DX = 16
DY = 8
LX = 4
LY = 3
ROWS = 8
CHUNKS = 2
EARLY = 12
LANES = 128
MESH = pl.DeviceIdType.MESH


def node_list():
    return (1.0 - np.cos(np.pi * (2.0 * np.arange(Q) + 1.0) / (2.0 * Q))) / 2.0


def cheb_table(child_half):
    nodes = node_list()
    targets = (child_half + nodes) / 2.0
    table = np.ones((Q, Q))
    for m in range(Q):
        for n in range(Q):
            if n != m:
                table[:, m] = table[:, m] * (targets - nodes[n]) / (nodes[m] - nodes[n])
    return table


def pick(index, values):
    total = jnp.full(index.shape, float(values[0]), jnp.float32)
    for k in range(1, len(values)):
        total = jnp.where(index == k, float(values[k]), total)
    return total


def fill_weights(axis, high_ref, low_ref):
    nodes = node_list()
    scale = [1.0 / np.prod([nodes[m] - nodes[n] for n in range(Q) if n != m]) for m in range(Q)]
    shape = (LANES, 2 * LANES)
    source = lax.broadcasted_iota(jnp.int32, (LANES, 1), 0)
    target = lax.broadcasted_iota(jnp.int32, (1, 2 * LANES), 1)
    first, second = source // Q % Q, source % Q
    t_first, t_second = target // Q % Q, target % Q
    child = (target // LANES).astype(jnp.float32)
    if axis == 0:
        own, other, t_own, t_other = first, second, t_first, t_second
    else:
        own, other, t_own, t_other = second, first, t_second, t_first
    place = (child + pick(t_own, nodes)) * 0.5
    table = jnp.broadcast_to(pick(own, scale), shape)
    for n in range(Q):
        table = table * jnp.where(own == n, 1.0, place - float(nodes[n]))
    group = source // (Q * Q) * Q + other
    t_group = target % LANES // (Q * Q) * Q + t_other
    table = jnp.where(group == t_group, table, 0.0)
    high = table.astype(jnp.bfloat16)
    high_ref[0:LANES, :] = high
    high_ref[LANES : 2 * LANES, :] = high
    low_ref[...] = (table - high.astype(jnp.float32)).astype(jnp.bfloat16)


def fit(function, count, odd):
    r = 0.5 * np.cos(np.pi * (np.arange(400) + 0.5) / 800)
    basis = np.stack([r ** (2 * k + (1 if odd else 0)) for k in range(count)], axis=1)
    return [float(c) for c in np.linalg.lstsq(basis, function(r), rcond=None)[0]]


SIN_FIT = fit(lambda r: 2.0 * np.sin(np.pi * r), 5, True)
COS_FIT = fit(lambda r: np.cos(np.pi * r), 5, False)


def horner(coefs, z):
    total = coefs[-1] * z + coefs[-2]
    for c in coefs[-3::-1]:
        total = total * z + c
    return total


def turn(cycles):
    r = cycles - jnp.round(cycles)
    z = r * r
    twice_sine = horner(SIN_FIT, z) * r
    cosine = horner(COS_FIT, z)
    return 1.0 - 0.5 * (twice_sine * twice_sine), twice_sine * cosine


def root(v):
    inverse = lax.rsqrt(v)
    s = v * inverse
    return s + (0.5 * inverse) * (v - s * s), inverse


def with_linear(cosine, sine, lin_cos, lin_sin):
    rc = cosine * lin_cos
    ss = sine * lin_sin
    rs = cosine * lin_sin
    sc = sine * lin_cos
    return rc + ss, sc - rs, rc - ss, sc + rs


def kernel(
    x_hbm,
    out_ref,
    x_ref,
    wx_high,
    wx_low,
    wy_high,
    wy_low,
    send_buf,
    recv_buf,
    state_a,
    state_b,
    fin,
    tw_x,
    tw_y0,
    tw_y1,
    tw_y2,
    c2_tab,
    load_sem,
    send_sem,
    recv_sem,
    row_sem,
):
    ix = lax.axis_index("sx")
    iy = lax.axis_index("sy")
    slots = DX * DY

    load = pltpu.make_async_copy(x_hbm, x_ref, load_sem)
    load.start()

    barrier = pltpu.get_barrier_semaphore()

    def other_x(j):
        return lax.rem(ix + j, DX)

    def other_y(j):
        return lax.rem(iy + j, DY)

    def greet(semaphore, device):
        pl.semaphore_signal(semaphore, inc=1, device_id=device, device_id_type=MESH)

    for j in range(1, DX):
        greet(barrier, (other_x(j), iy))
    for j in range(1, DY):
        greet(barrier, (ix, other_y(j)))

    def pack(dx):
        for part in range(2):
            halves = [
                x_ref[pl.ds(part * 2048 + 2 * dx + g, Q * Q, stride=32), :] for g in range(2)
            ]
            turned = jnp.concatenate(halves, axis=0).T
            for dy in range(DY):
                for c in range(CHUNKS):
                    low = (dy * CHUNKS + c) * ROWS
                    send_buf[c, dx * DY + dy, part] = turned[low : low + ROWS]

    def send(c, dx, dy):
        pltpu.make_async_remote_copy(
            src_ref=send_buf.at[c, dx * DY + dy],
            dst_ref=recv_buf.at[c, iy * DX + ix],
            send_sem=send_sem.at[c],
            recv_sem=recv_sem.at[c],
            device_id=(dx, dy),
            device_id_type=MESH,
        ).start()

    def sent(c):
        return pltpu.make_async_remote_copy(
            src_ref=send_buf.at[c, pl.ds(0, slots - 1)],
            dst_ref=recv_buf.at[c, pl.ds(0, slots - 1)],
            send_sem=send_sem.at[c],
            recv_sem=recv_sem.at[c],
            device_id=(ix, iy),
            device_id_type=MESH,
        )

    def pack_all(j, carry):
        pack(other_x(j))
        return carry

    def pack_column(j, carry):
        pack(other_x(j))
        send(0, other_x(j), iy)
        return carry

    def send_column(j, carry):
        send(0, other_x(j), iy)
        return carry

    def send_rest(j, carry):
        for k in range(1, DY):
            send(0, other_x(j), other_y(k))
        return carry

    load.wait()
    lax.fori_loop(0, EARLY, pack_all, 0)
    for c in range(CHUNKS):
        recv_buf[c, iy * DX + ix] = send_buf[c, ix * DY + iy]
    pl.semaphore_wait(barrier, DX + DY - 2)
    for j in range(1, DY):
        greet(row_sem, (ix, other_y(j)))
    for j in range(1, DY):
        send(0, ix, other_y(j))
    lax.fori_loop(1, EARLY, send_column, 0)
    if EARLY < DX:
        lax.fori_loop(EARLY, DX, pack_column, 0)
    pl.semaphore_wait(row_sem, DY - 1)
    lax.fori_loop(1, DX, send_rest, 0)

    fill_weights(0, wx_high, wx_low)
    fill_weights(1, wy_high, wy_low)
    nodes = node_list()
    angles = 2.0 * np.pi * nodes
    lane = lax.broadcasted_iota(jnp.int32, (1, LANES), 1)
    t_one, t_two = lane // Q % Q, lane % Q
    z_one, z_two = pick(t_one, nodes), pick(t_two, nodes)
    cos_one, sin_one = pick(t_one, np.cos(angles)), pick(t_one, np.sin(angles))
    cos_two, sin_two = pick(t_two, np.cos(angles)), pick(t_two, np.sin(angles))
    g_bit = (lane // (Q * Q)).astype(jnp.float32)
    row = lax.broadcasted_iota(jnp.int32, (ROWS, LANES), 0).astype(jnp.float32)
    base_one = (2 * ix).astype(jnp.float32) + g_bit

    def place_one(level, h):
        box = base_one * float(2 << level) + h.astype(jnp.float32)
        count = DX >> (level + 1)
        return jnp.broadcast_to((box + z_one) * (4.0 * count / N), (ROWS, LANES))

    def place_two(c, level, h):
        box = (row + (iy * (CHUNKS * ROWS) + c * ROWS).astype(jnp.float32)) * float(1 << level) + float(h)
        count = DY >> level
        return (box + z_two) * (4.0 * count / N)

    for level in range(LX):
        count = DX >> level
        width = N // count
        fans = 2 << level

        def x_twiddles(step, carry, level=level, count=count, width=width, fans=fans):
            c = step // fans
            h = lax.rem(step, fans)
            c1, s1 = turn(place_one(level, h))
            c2, s2 = turn(place_two(c, 0, 0))
            speed_one = (2.0 + s1 * s2) * (1.0 / 16.0)
            speed_two = (2.0 + c1 * c2) * (1.0 / 16.0)
            square_one = speed_one * speed_one
            square_two = speed_two * speed_two
            for u2 in range(DY // 2):
                k2 = (u2 + 0.5) * (N / DY) - 0.5 * N
                second = square_two * (k2 * k2)
                parents = {}
                for u1 in range(count // 2):
                    child = (u1 + 0.5) * width - 0.5 * N
                    parent = (u1 // 2 + 0.5) * (2 * width) - 0.5 * N
                    if parent not in parents:
                        parents[parent] = root(square_one * (parent * parent) + second)[0]
                    s_parent = parents[parent]
                    s_child, _ = root(square_one * (child * child) + second)
                    total = s_child + s_parent
                    gap = square_one * (child * child - parent * parent) / total
                    cosine, sine = turn(gap)
                    four = with_linear(cosine, sine, cos_one, sin_one)
                    for k in range(4):
                        tw_x[level, c, u2, u1 * fans + h, k] = four[k]
            return carry

        lax.fori_loop(0, CHUNKS * fans, x_twiddles, 0)

    for c in range(CHUNKS):
        for level in range(LY):
            for h in range(2 << level):
                cosine, _ = turn(place_two(c, level + 1, h))
                c2_tab[c, (2 << level) - 2 + h] = cosine

    tw_y = (tw_y0, tw_y1, tw_y2)

    def y_twiddles(step, carry):
        c = step // DX
        h = lax.rem(step, DX)
        c1, _ = turn(place_one(LX - 1, h))
        for level in range(LY):
            for k in range(2 << level):
                gap = c1 * c2_tab[c, (2 << level) - 2 + k] * float((N // 16 << level) // 16)
                cosine, sine = turn(gap)
                four = with_linear(cosine, sine, cos_two, sin_two)
                for q in range(4):
                    tw_y[level][c, h, k, q] = four[q]
        return carry

    lax.fori_loop(0, CHUNKS * DX, y_twiddles, 0)

    sent(0).wait_send()

    def send_second(j, carry):
        send(1, other_x(j // DY), other_y(lax.rem(j, DY)))
        return carry

    lax.fori_loop(1, slots, send_second, 0)

    def spread(block, high_ref, low_ref):
        high = block.astype(jnp.bfloat16)
        low = (block - high.astype(jnp.float32)).astype(jnp.bfloat16)
        both = jnp.concatenate([high, low], axis=1)
        main = jnp.dot(both, high_ref[...], preferred_element_type=jnp.float32)
        return main + jnp.dot(high, low_ref[...], preferred_element_type=jnp.float32)

    def levels(c, carry):
        sent(c).wait_recv()

        for level in range(LX):
            count = DX >> level
            fans = 1 << level
            source = (None, state_a, state_b, state_a)[level]
            target = (state_a, state_b, state_a, state_b)[level]

            def x_level(b2, carry, level=level, count=count, fans=fans, source=source, target=target):
                if level == 0:
                    block = recv_buf[c, pl.ds(b2 * DX, DX)]
                else:
                    block = source[pl.ds(b2 * DX, DX)]
                wide = spread(block.reshape(DX * 2 * ROWS, LANES), wx_high, wx_low)
                u2 = jnp.minimum(b2, DY - 1 - b2)
                for parent in range(count // 2):
                    for old in range(fans):
                        for h in range(2):
                            fan = 2 * old + h
                            re = im = None
                            for bit in range(2):
                                b1 = 2 * parent + bit
                                u1 = min(b1, count - 1 - b1)
                                low = (b1 * fans + old) * 2 * ROWS
                                a_re = wide[low : low + ROWS, h * LANES : (h + 1) * LANES]
                                a_im = wide[low + ROWS : low + 2 * ROWS, h * LANES : (h + 1) * LANES]
                                t_re = tw_x[level, c, u2, u1 * 2 * fans + fan, 2 * bit]
                                t_im = tw_x[level, c, u2, u1 * 2 * fans + fan, 2 * bit + 1]
                                n_re = a_re * t_re - a_im * t_im
                                n_im = a_re * t_im + a_im * t_re
                                re = n_re if re is None else re + n_re
                                im = n_im if im is None else im + n_im
                            slot = parent * 2 * fans + fan
                            if level == LX - 1:
                                target[slot * DY + b2, 0] = re
                                target[slot * DY + b2, 1] = im
                            else:
                                target[b2 * DX + slot, 0] = re
                                target[b2 * DX + slot, 1] = im
                return carry

            lax.fori_loop(0, DY, x_level, 0, unroll=True)

        for level in range(LY):
            count = DY >> level
            fans = 1 << level
            source = (state_b, state_a, state_b)[level]
            target = (state_a, state_b, None)[level]
            table = tw_y[level]

            def y_level(pair, carry, level=level, count=count, fans=fans, source=source, target=target, table=table):
                block = source[pl.ds(pair * 2 * DY, 2 * DY)]
                wide = spread(block.reshape(2 * DY * 2 * ROWS, LANES), wy_high, wy_low)
                for which in range(2):
                    hx = pair * 2 + which
                    for old in range(fans):
                        for h in range(2):
                            fan = 2 * old + h
                            u_re, u_im, w_re, w_im = (table[c, hx, fan, q] for q in range(4))
                            cut = slice(h * LANES, (h + 1) * LANES)
                            for parent in range(count // 2):
                                low_a = (which * DY + 2 * parent * fans + old) * 2 * ROWS
                                low_b = (which * DY + (2 * parent + 1) * fans + old) * 2 * ROWS
                                a_re = wide[low_a : low_a + ROWS, cut]
                                a_im = wide[low_a + ROWS : low_a + 2 * ROWS, cut]
                                b_re = wide[low_b : low_b + ROWS, cut]
                                b_im = wide[low_b + ROWS : low_b + 2 * ROWS, cut]
                                if level == LY - 1:
                                    re = (a_re * u_re - a_im * u_im) + (b_re * w_re - b_im * w_im)
                                    im = (a_re * u_im + a_im * u_re) + (b_re * w_im + b_im * w_re)
                                elif parent < count // 4:
                                    re = (a_re + b_re) * u_re - (a_im - b_im) * u_im
                                    im = (a_im + b_im) * u_re + (a_re - b_re) * u_im
                                else:
                                    re = (a_re + b_re) * w_re + (a_im - b_im) * w_im
                                    im = (a_im + b_im) * w_re - (a_re - b_re) * w_im
                                if level == LY - 1:
                                    fin[0, hx, pl.ds(c * (ROWS * DY) + fan, ROWS, stride=DY), :] = re
                                    fin[1, hx, pl.ds(c * (ROWS * DY) + fan, ROWS, stride=DY), :] = im
                                else:
                                    slot = hx * DY + parent * 2 * fans + fan
                                    target[slot, 0] = re
                                    target[slot, 1] = im
                return carry

            lax.fori_loop(0, DX // 2, y_level, 0, unroll=True)
        return carry

    lax.fori_loop(0, CHUNKS, levels, 0)

    def unpack(hx, carry):
        for part in range(2):
            turned = fin[part, hx].T
            for g in range(2):
                out_ref[pl.ds(part * 2048 + g * DX + hx, Q * Q, stride=32), :] = turned[
                    g * Q * Q : (g + 1) * Q * Q
                ]
        return carry

    lax.fori_loop(0, DX, unpack, 0, unroll=4)

    sent(1).wait_send()


def local(coeffs):
    rows = 2 * Q * Q * 32
    flat = pltpu.with_memory_space_constraint(jnp.reshape(coeffs, (rows, LANES)), pltpu.HBM)
    slots = DX * DY
    f32 = jnp.float32
    out = pl.pallas_call(
        kernel,
        out_shape=jax.ShapeDtypeStruct((rows, LANES), f32),
        in_specs=[pl.BlockSpec(memory_space=pltpu.HBM)],
        out_specs=pl.BlockSpec(memory_space=pltpu.VMEM),
        scratch_shapes=[
            pltpu.VMEM((rows, LANES), f32),
            pltpu.VMEM((2 * LANES, 2 * LANES), jnp.bfloat16),
            pltpu.VMEM((LANES, 2 * LANES), jnp.bfloat16),
            pltpu.VMEM((2 * LANES, 2 * LANES), jnp.bfloat16),
            pltpu.VMEM((LANES, 2 * LANES), jnp.bfloat16),
            pltpu.VMEM((CHUNKS, slots, 2, ROWS, LANES), f32),
            pltpu.VMEM((CHUNKS, slots, 2, ROWS, LANES), f32),
            pltpu.VMEM((slots, 2, ROWS, LANES), f32),
            pltpu.VMEM((slots, 2, ROWS, LANES), f32),
            pltpu.VMEM((2, DX, LANES, LANES), f32),
            pltpu.VMEM((LX, CHUNKS, DY // 2, DX, 4, ROWS, LANES), f32),
            pltpu.VMEM((CHUNKS, DX, 2, 4, ROWS, LANES), f32),
            pltpu.VMEM((CHUNKS, DX, 4, 4, ROWS, LANES), f32),
            pltpu.VMEM((CHUNKS, DX, 8, 4, ROWS, LANES), f32),
            pltpu.VMEM((CHUNKS, 14, ROWS, LANES), f32),
            pltpu.SemaphoreType.DMA,
            pltpu.SemaphoreType.DMA((CHUNKS,)),
            pltpu.SemaphoreType.DMA((CHUNKS,)),
            pltpu.SemaphoreType.REGULAR,
        ],
        compiler_params=pltpu.CompilerParams(
            collective_id=0, has_side_effects=True, vmem_limit_bytes=32 << 20
        ),
        name="butterfly",
    )(flat)
    return jnp.reshape(out, (2, Q, Q, 32, LANES))


def solution(mesh):
    in_specs = (P(None, None, None, "sx", "sy", None, None),)
    out_specs = P(None, None, None, "sx", "sy")
    return jax.shard_map(local, mesh=mesh, in_specs=in_specs, out_specs=out_specs, check_vma=False)
```

```python
import functools
import math

import jax
import jax.numpy as jnp
import numpy as np
from jax import lax
from jax.experimental import pallas as pl
from jax.experimental.pallas import tpu as pltpu
from jax.sharding import PartitionSpec as P

N = 8192
Q = 8
DX = 16
DY = 8
LX = 4
LY = 3
ROWS = 8
CHUNKS = 2
EARLY = 12
LANES = 128
MESH = pl.DeviceIdType.MESH


def node_list():
    return (1.0 - np.cos(np.pi * (2.0 * np.arange(Q) + 1.0) / (2.0 * Q))) / 2.0


def cheb_table(child_half):
    nodes = node_list()
    targets = (child_half + nodes) / 2.0
    table = np.ones((Q, Q))
    for m in range(Q):
        for n in range(Q):
            if n != m:
                table[:, m] = table[:, m] * (targets - nodes[n]) / (nodes[m] - nodes[n])
    return table


def pick(index, values):
    total = jnp.full(index.shape, float(values[0]), jnp.float32)
    for k in range(1, len(values)):
        total = jnp.where(index == k, float(values[k]), total)
    return total


def fill_weights(axis, high_ref, low_ref):
    nodes = node_list()
    scale = [1.0 / np.prod([nodes[m] - nodes[n] for n in range(Q) if n != m]) for m in range(Q)]
    shape = (LANES, 2 * LANES)
    source = lax.broadcasted_iota(jnp.int32, (LANES, 1), 0)
    target = lax.broadcasted_iota(jnp.int32, (1, 2 * LANES), 1)
    first, second = source // Q % Q, source % Q
    t_first, t_second = target // Q % Q, target % Q
    child = (target // LANES).astype(jnp.float32)
    if axis == 0:
        own, other, t_own, t_other = first, second, t_first, t_second
    else:
        own, other, t_own, t_other = second, first, t_second, t_first
    place = (child + pick(t_own, nodes)) * 0.5
    table = jnp.broadcast_to(pick(own, scale), shape)
    for n in range(Q):
        table = table * jnp.where(own == n, 1.0, place - float(nodes[n]))
    group = source // (Q * Q) * Q + other
    t_group = target % LANES // (Q * Q) * Q + t_other
    table = jnp.where(group == t_group, table, 0.0)
    high = table.astype(jnp.bfloat16)
    high_ref[0:LANES, :] = high
    high_ref[LANES : 2 * LANES, :] = high
    low_ref[...] = (table - high.astype(jnp.float32)).astype(jnp.bfloat16)


def fit(function, count, odd):
    r = 0.5 * np.cos(np.pi * (np.arange(400) + 0.5) / 800)
    basis = np.stack([r ** (2 * k + (1 if odd else 0)) for k in range(count)], axis=1)
    return [float(c) for c in np.linalg.lstsq(basis, function(r), rcond=None)[0]]


SIN_FIT = fit(lambda r: 2.0 * np.sin(np.pi * r), 5, True)
COS_FIT = fit(lambda r: np.cos(np.pi * r), 5, False)


def horner(coefs, z):
    total = coefs[-1] * z + coefs[-2]
    for c in coefs[-3::-1]:
        total = total * z + c
    return total


def turn(cycles):
    r = cycles - jnp.round(cycles)
    z = r * r
    twice_sine = horner(SIN_FIT, z) * r
    cosine = horner(COS_FIT, z)
    return 1.0 - 0.5 * (twice_sine * twice_sine), twice_sine * cosine


def root(v):
    inverse = lax.rsqrt(v)
    s = v * inverse
    return s + (0.5 * inverse) * (v - s * s), inverse


def with_linear(cosine, sine, lin_cos, lin_sin):
    rc = cosine * lin_cos
    ss = sine * lin_sin
    rs = cosine * lin_sin
    sc = sine * lin_cos
    return rc + ss, sc - rs, rc - ss, sc + rs


def kernel(
    x_hbm,
    out_ref,
    x_ref,
    wx_high,
    wx_low,
    wy_high,
    wy_low,
    send_buf,
    recv_buf,
    state_a,
    state_b,
    fin,
    tw_x,
    tw_y0,
    tw_y1,
    tw_y2,
    c2_tab,
    load_sem,
    send_sem,
    recv_sem,
    row_sem,
):
    ix = lax.axis_index("sx")
    iy = lax.axis_index("sy")
    slots = DX * DY

    load = pltpu.make_async_copy(x_hbm, x_ref, load_sem)
    load.start()

    barrier = pltpu.get_barrier_semaphore()

    def other_x(j):
        return lax.rem(ix + j, DX)

    def other_y(j):
        return lax.rem(iy + j, DY)

    def greet(semaphore, device):
        pl.semaphore_signal(semaphore, inc=1, device_id=device, device_id_type=MESH)

    for j in range(1, DX):
        greet(barrier, (other_x(j), iy))
    for j in range(1, DY):
        greet(barrier, (ix, other_y(j)))

    def pack(dx):
        for part in range(2):
            halves = [
                x_ref[pl.ds(part * 2048 + 2 * dx + g, Q * Q, stride=32), :] for g in range(2)
            ]
            turned = jnp.concatenate(halves, axis=0).T
            for dy in range(DY):
                for c in range(CHUNKS):
                    low = (dy * CHUNKS + c) * ROWS
                    send_buf[c, dx * DY + dy, part] = turned[low : low + ROWS]

    def send(c, dx, dy):
        pltpu.make_async_remote_copy(
            src_ref=send_buf.at[c, dx * DY + dy],
            dst_ref=recv_buf.at[c, iy * DX + ix],
            send_sem=send_sem.at[c],
            recv_sem=recv_sem.at[c],
            device_id=(dx, dy),
            device_id_type=MESH,
        ).start()

    def sent(c):
        return pltpu.make_async_remote_copy(
            src_ref=send_buf.at[c, pl.ds(0, slots - 1)],
            dst_ref=recv_buf.at[c, pl.ds(0, slots - 1)],
            send_sem=send_sem.at[c],
            recv_sem=recv_sem.at[c],
            device_id=(ix, iy),
            device_id_type=MESH,
        )

    def pack_all(j, carry):
        pack(other_x(j))
        return carry

    def pack_column(j, carry):
        pack(other_x(j))
        send(0, other_x(j), iy)
        return carry

    def send_column(j, carry):
        send(0, other_x(j), iy)
        return carry

    def send_rest(j, carry):
        for k in range(1, DY):
            send(0, other_x(j), other_y(k))
        return carry

    load.wait()
    lax.fori_loop(0, EARLY, pack_all, 0)
    for c in range(CHUNKS):
        recv_buf[c, iy * DX + ix] = send_buf[c, ix * DY + iy]
    pl.semaphore_wait(barrier, DX + DY - 2)
    for j in range(1, DY):
        greet(row_sem, (ix, other_y(j)))
    for j in range(1, DY):
        send(0, ix, other_y(j))
    lax.fori_loop(1, EARLY, send_column, 0)
    if EARLY < DX:
        lax.fori_loop(EARLY, DX, pack_column, 0)
    pl.semaphore_wait(row_sem, DY - 1)
    lax.fori_loop(1, DX, send_rest, 0)

    fill_weights(0, wx_high, wx_low)
    fill_weights(1, wy_high, wy_low)
    nodes = node_list()
    angles = 2.0 * np.pi * nodes
    lane = lax.broadcasted_iota(jnp.int32, (1, LANES), 1)
    t_one, t_two = lane // Q % Q, lane % Q
    z_one, z_two = pick(t_one, nodes), pick(t_two, nodes)
    cos_one, sin_one = pick(t_one, np.cos(angles)), pick(t_one, np.sin(angles))
    cos_two, sin_two = pick(t_two, np.cos(angles)), pick(t_two, np.sin(angles))
    g_bit = (lane // (Q * Q)).astype(jnp.float32)
    row = lax.broadcasted_iota(jnp.int32, (ROWS, LANES), 0).astype(jnp.float32)
    base_one = (2 * ix).astype(jnp.float32) + g_bit

    def place_one(level, h):
        box = base_one * float(2 << level) + h.astype(jnp.float32)
        count = DX >> (level + 1)
        return jnp.broadcast_to((box + z_one) * (4.0 * count / N), (ROWS, LANES))

    def place_two(c, level, h):
        box = (row + (iy * (CHUNKS * ROWS) + c * ROWS).astype(jnp.float32)) * float(1 << level) + float(h)
        count = DY >> level
        return (box + z_two) * (4.0 * count / N)

    for level in range(LX):
        count = DX >> level
        width = N // count
        fans = 2 << level

        def x_twiddles(step, carry, level=level, count=count, width=width, fans=fans):
            c = step // fans
            h = lax.rem(step, fans)
            c1, s1 = turn(place_one(level, h))
            c2, s2 = turn(place_two(c, 0, 0))
            speed_one = (2.0 + s1 * s2) * (1.0 / 16.0)
            speed_two = (2.0 + c1 * c2) * (1.0 / 16.0)
            square_one = speed_one * speed_one
            square_two = speed_two * speed_two
            for u2 in range(DY // 2):
                k2 = (u2 + 0.5) * (N / DY) - 0.5 * N
                second = square_two * (k2 * k2)
                parents = {}
                for u1 in range(count // 2):
                    child = (u1 + 0.5) * width - 0.5 * N
                    parent = (u1 // 2 + 0.5) * (2 * width) - 0.5 * N
                    if parent not in parents:
                        parents[parent] = root(square_one * (parent * parent) + second)[0]
                    s_parent = parents[parent]
                    s_child, _ = root(square_one * (child * child) + second)
                    total = s_child + s_parent
                    gap = square_one * (child * child - parent * parent) / total
                    cosine, sine = turn(gap)
                    four = with_linear(cosine, sine, cos_one, sin_one)
                    for k in range(4):
                        tw_x[level, c, u2, u1 * fans + h, k] = four[k]
            return carry

        lax.fori_loop(0, CHUNKS * fans, x_twiddles, 0)

    for c in range(CHUNKS):
        for level in range(LY):
            for h in range(2 << level):
                cosine, _ = turn(place_two(c, level + 1, h))
                c2_tab[c, (2 << level) - 2 + h] = cosine

    tw_y = (tw_y0, tw_y1, tw_y2)

    def y_twiddles(step, carry):
        c = step // DX
        h = lax.rem(step, DX)
        c1, _ = turn(place_one(LX - 1, h))
        for level in range(LY):
            for k in range(2 << level):
                gap = c1 * c2_tab[c, (2 << level) - 2 + k] * float((N // 16 << level) // 16)
                cosine, sine = turn(gap)
                four = with_linear(cosine, sine, cos_two, sin_two)
                for q in range(4):
                    tw_y[level][c, h, k, q] = four[q]
        return carry

    lax.fori_loop(0, CHUNKS * DX, y_twiddles, 0)

    sent(0).wait_send()

    def send_second(j, carry):
        send(1, other_x(j // DY), other_y(lax.rem(j, DY)))
        return carry

    lax.fori_loop(1, slots, send_second, 0)

    def spread(block, high_ref, low_ref):
        high = block.astype(jnp.bfloat16)
        low = (block - high.astype(jnp.float32)).astype(jnp.bfloat16)
        both = jnp.concatenate([high, low], axis=1)
        main = jnp.dot(both, high_ref[...], preferred_element_type=jnp.float32)
        return main + jnp.dot(high, low_ref[...], preferred_element_type=jnp.float32)

    def unpack(hx, carry):
        for part in range(2):
            turned = fin[part, hx].T
            for g in range(2):
                out_ref[pl.ds(part * 2048 + g * DX + hx, Q * Q, stride=32), :] = turned[
                    g * Q * Q : (g + 1) * Q * Q
                ]
        return carry

    def levels(c, carry):
        sent(c).wait_recv()

        for level in range(LX):
            count = DX >> level
            fans = 1 << level
            source = (None, state_a, state_b, state_a)[level]
            target = (state_a, state_b, state_a, state_b)[level]

            def x_level(b2, carry, level=level, count=count, fans=fans, source=source, target=target):
                if level == 0:
                    block = recv_buf[c, pl.ds(b2 * DX, DX)]
                else:
                    block = source[pl.ds(b2 * DX, DX)]
                wide = spread(block.reshape(DX * 2 * ROWS, LANES), wx_high, wx_low)
                u2 = min(b2, DY - 1 - b2)
                for parent in range(count // 2):
                    for old in range(fans):
                        for h in range(2):
                            fan = 2 * old + h
                            re = im = None
                            for bit in range(2):
                                b1 = 2 * parent + bit
                                u1 = min(b1, count - 1 - b1)
                                low = (b1 * fans + old) * 2 * ROWS
                                a_re = wide[low : low + ROWS, h * LANES : (h + 1) * LANES]
                                a_im = wide[low + ROWS : low + 2 * ROWS, h * LANES : (h + 1) * LANES]
                                t_re = tw_x[level, c, u2, u1 * 2 * fans + fan, 2 * bit]
                                t_im = tw_x[level, c, u2, u1 * 2 * fans + fan, 2 * bit + 1]
                                n_re = a_re * t_re - a_im * t_im
                                n_im = a_re * t_im + a_im * t_re
                                re = n_re if re is None else re + n_re
                                im = n_im if im is None else im + n_im
                            slot = parent * 2 * fans + fan
                            if level == LX - 1:
                                target[slot * DY + b2, 0] = re
                                target[slot * DY + b2, 1] = im
                            else:
                                target[b2 * DX + slot, 0] = re
                                target[b2 * DX + slot, 1] = im
                return carry

            for b2 in range(DY):
                x_level(b2, 0)

        for level in range(LY):
            count = DY >> level
            fans = 1 << level
            source = (state_b, state_a, state_b)[level]
            target = (state_a, state_b, None)[level]
            table = tw_y[level]

            def y_level(pair, carry, level=level, count=count, fans=fans, source=source, target=target, table=table):
                block = source[pl.ds(pair * 2 * DY, 2 * DY)]
                wide = spread(block.reshape(2 * DY * 2 * ROWS, LANES), wy_high, wy_low)
                for which in range(2):
                    hx = pair * 2 + which
                    for old in range(fans):
                        for h in range(2):
                            fan = 2 * old + h
                            u_re, u_im, w_re, w_im = (table[c, hx, fan, q] for q in range(4))
                            cut = slice(h * LANES, (h + 1) * LANES)
                            for parent in range(count // 2):
                                low_a = (which * DY + 2 * parent * fans + old) * 2 * ROWS
                                low_b = (which * DY + (2 * parent + 1) * fans + old) * 2 * ROWS
                                a_re = wide[low_a : low_a + ROWS, cut]
                                a_im = wide[low_a + ROWS : low_a + 2 * ROWS, cut]
                                b_re = wide[low_b : low_b + ROWS, cut]
                                b_im = wide[low_b + ROWS : low_b + 2 * ROWS, cut]
                                if level == LY - 1:
                                    re = (a_re * u_re - a_im * u_im) + (b_re * w_re - b_im * w_im)
                                    im = (a_re * u_im + a_im * u_re) + (b_re * w_im + b_im * w_re)
                                elif parent < count // 4:
                                    re = (a_re + b_re) * u_re - (a_im - b_im) * u_im
                                    im = (a_im + b_im) * u_re + (a_re - b_re) * u_im
                                else:
                                    re = (a_re + b_re) * w_re + (a_im - b_im) * w_im
                                    im = (a_im + b_im) * w_re - (a_re - b_re) * w_im
                                if level == LY - 1:
                                    fin[0, hx, pl.ds(c * (ROWS * DY) + fan, ROWS, stride=DY), :] = re
                                    fin[1, hx, pl.ds(c * (ROWS * DY) + fan, ROWS, stride=DY), :] = im
                                else:
                                    slot = hx * DY + parent * 2 * fans + fan
                                    target[slot, 0] = re
                                    target[slot, 1] = im
                    if level == LY - 1 and c == CHUNKS - 1:
                        unpack(hx, 0)
                return carry

            for pair in range(DX // 2):
                y_level(pair, 0)
        return carry

    for c in range(CHUNKS):
        levels(c, 0)

    sent(1).wait_send()


def local(coeffs):
    rows = 2 * Q * Q * 32
    flat = pltpu.with_memory_space_constraint(jnp.reshape(coeffs, (rows, LANES)), pltpu.HBM)
    slots = DX * DY
    f32 = jnp.float32
    out = pl.pallas_call(
        kernel,
        out_shape=jax.ShapeDtypeStruct((rows, LANES), f32),
        in_specs=[pl.BlockSpec(memory_space=pltpu.HBM)],
        out_specs=pl.BlockSpec(memory_space=pltpu.VMEM),
        scratch_shapes=[
            pltpu.VMEM((rows, LANES), f32),
            pltpu.VMEM((2 * LANES, 2 * LANES), jnp.bfloat16),
            pltpu.VMEM((LANES, 2 * LANES), jnp.bfloat16),
            pltpu.VMEM((2 * LANES, 2 * LANES), jnp.bfloat16),
            pltpu.VMEM((LANES, 2 * LANES), jnp.bfloat16),
            pltpu.VMEM((CHUNKS, slots, 2, ROWS, LANES), f32),
            pltpu.VMEM((CHUNKS, slots, 2, ROWS, LANES), f32),
            pltpu.VMEM((slots, 2, ROWS, LANES), f32),
            pltpu.VMEM((slots, 2, ROWS, LANES), f32),
            pltpu.VMEM((2, DX, LANES, LANES), f32),
            pltpu.VMEM((LX, CHUNKS, DY // 2, DX, 4, ROWS, LANES), f32),
            pltpu.VMEM((CHUNKS, DX, 2, 4, ROWS, LANES), f32),
            pltpu.VMEM((CHUNKS, DX, 4, 4, ROWS, LANES), f32),
            pltpu.VMEM((CHUNKS, DX, 8, 4, ROWS, LANES), f32),
            pltpu.VMEM((CHUNKS, 14, ROWS, LANES), f32),
            pltpu.SemaphoreType.DMA,
            pltpu.SemaphoreType.DMA((CHUNKS,)),
            pltpu.SemaphoreType.DMA((CHUNKS,)),
            pltpu.SemaphoreType.REGULAR,
        ],
        compiler_params=pltpu.CompilerParams(
            collective_id=0, has_side_effects=True, vmem_limit_bytes=32 << 20
        ),
        name="butterfly",
    )(flat)
    return jnp.reshape(out, (2, Q, Q, 32, LANES))


def solution(mesh):
    in_specs = (P(None, None, None, "sx", "sy", None, None),)
    out_specs = P(None, None, None, "sx", "sy")
    return jax.shard_map(local, mesh=mesh, in_specs=in_specs, out_specs=out_specs, check_vma=False)
```
